32 devices in a mesh: grp: 2 (over y), seq: 4 (over z), sub: 4 (over x, core).
Axes of the slice: x: 2, y: 2, z: 4, core: 2. Of those that a mesh axis runs over, the one named last changes fastest.
Arguments:
- activations: bfloat16 [32768, 384], P(('grp', 'seq', 'sub')), parts along dimension 0, may hold values from -6 to 6
- cotangent: bfloat16 [32768, 384], P(('grp', 'seq', 'sub')), parts along dimension 0, may hold values from -6 to 6
- weights: bfloat16 [2304, 384], P('sub'), may hold values from -0.1875 to 0.1875
Outputs:
- input_grad: bfloat16 [32768, 384], P(('grp', 'seq', 'sub')), parts along dimension 0
- weight_grad: float32 [4608, 384], P(('grp', 'sub')), parts along dimension 0
The draws below stay inside these ranges and needn't reach their ends.
There are 2 independent parts, one for each index of `grp`. The reference program is written for one: setup_inputs(seed, part) draws one part's arguments, and reference() takes and returns one part's arrays. A program takes and returns all parts, laid end to end along the dimension named above; an argument that names none is the same for every part. Nothing has to cross between parts.
All inputs are finite; a program needn't handle non-finite values.
Results may differ from the reference program's by a relative error of at most 0.0053.
Values may be sent and summed in bfloat16 or wider, within the bound.
A program may use at most 64 MiB of HBM per device.

```python
import math
import jax
import jax.numpy as jnp

C = 384
DILATION_FIRST = 1024
DILATION_SECOND = 2048
POSITIONS = 16384


def spiked(result, own_key, source, target, blocks, factor):
    def block_of(dim):
        return (jnp.arange(result.shape[dim]) // (result.shape[dim] // blocks)).reshape((-1,) + (1,) * (result.ndim - 1 - dim))

    near = jax.random.permutation(own_key, blocks)[block_of(target)]
    far = (block_of(target) + blocks // 2) % blocks
    return jnp.where((block_of(source) == near) | (block_of(source) == far), factor * result, result)


def shard_levels(own_key, dims, pieces, smallest, high):
    gain = 1.0
    for position, blocks in pieces:
        steps = jax.random.uniform(jax.random.fold_in(jax.random.fold_in(own_key, 6), position), (blocks,), jnp.float32, smallest / len(pieces), high / len(pieces))
        gain = gain * jnp.repeat(jnp.exp(steps), dims[position] // blocks).reshape((-1,) + (1,) * (len(dims) - 1 - position))
    return gain


def bell_draw(stream_key, shape, deviation, bound, shards=(), held_as=jnp.bfloat16):
    level = shard_levels(stream_key, shape, shards, -0.22, 0.18) if shards else 1.0
    entries = jax.random.normal(stream_key, shape, jnp.float32) * deviation * level
    return jnp.minimum(jnp.maximum(entries, -bound), bound).astype(held_as)


def noise_with(own_key, dims, deviation, most, shards, heavy, kind=jnp.bfloat16):
    result = deviation * jax.random.normal(own_key, dims, jnp.float32)
    if shards:
        result = result * shard_levels(own_key, dims, shards, -0.22, 0.18)
    return jnp.clip(spiked(result, jax.random.fold_in(own_key, 3), *heavy), -most, most).astype(kind)


def setup_inputs(seed: int = 0, part: int = 0) -> dict:
    streams_of = jax.random.split(jax.random.key(seed), 4)
    own_keys = jax.random.split(jax.random.fold_in(streams_of[3], part), 4)
    activations = noise_with(own_keys[0], (POSITIONS, C), 1.0, 6.0, ((0, 16),), (0, 1, 16, 2.0))
    cotangent = bell_draw(own_keys[1], (POSITIONS, C), 1.0, 6.0, ((0, 16),))
    weights = bell_draw(streams_of[2], (6 * C, C), (3 * C) ** -0.5, 0.1875, ((0, 4),))
    return dict(activations=activations, cotangent=cotangent, weights=weights)


def gelu_pair(pre_act):
    coeff = 0.7978845608
    tanh_value = jnp.tanh(coeff * (pre_act + 0.044715 * pre_act * pre_act * pre_act))
    gelu_value = 0.5 * pre_act * (1.0 + tanh_value)
    gelu_slope = 0.5 * (1.0 + tanh_value) + 0.5 * pre_act * (1.0 - tanh_value * tanh_value) * coeff * (1.0 + 3.0 * 0.044715 * pre_act * pre_act)
    return (gelu_value, gelu_slope)

def backward_shifted(source, distance):
    empty = jnp.zeros((distance, source.shape[1]), source.dtype)
    return jnp.concatenate((empty, source[:-distance]), 0)

def forward_shifted(source, distance):
    empty = jnp.zeros((distance, source.shape[1]), source.dtype)
    return jnp.concatenate((source[distance:], empty), 0)

def back_matrix(kernel):
    return kernel.reshape(3, C, C).transpose(0, 2, 1).reshape(3 * C, C)

def reference(activations, cotangent, weights):
    first = weights[:3 * C]
    second = weights[3 * C:]
    first_layer_weights = jnp.concatenate((backward_shifted(activations, DILATION_FIRST), activations, forward_shifted(activations, DILATION_FIRST)), 1)
    pre_one = jnp.dot(first_layer_weights, first, preferred_element_type=jnp.float32)
    gelu_one, slope_one = gelu_pair(pre_one)
    middle_state = (activations.astype(jnp.float32) + gelu_one).astype(jnp.bfloat16)
    second_layer_weights = jnp.concatenate((backward_shifted(middle_state, DILATION_SECOND), middle_state, forward_shifted(middle_state, DILATION_SECOND)), 1)
    pre_two = jnp.dot(second_layer_weights, second, preferred_element_type=jnp.float32)
    gelu_two, slope_two = gelu_pair(pre_two)
    second_error = (cotangent.astype(jnp.float32) * slope_two).astype(jnp.bfloat16)
    grad_scale = 1.0 / math.sqrt(POSITIONS)
    grad_two = jnp.dot(second_layer_weights.T, second_error, preferred_element_type=jnp.float32) * grad_scale
    second_reach = jnp.concatenate((forward_shifted(second_error, DILATION_SECOND), second_error, backward_shifted(second_error, DILATION_SECOND)), 1)
    back_one = cotangent.astype(jnp.float32) + jnp.dot(second_reach, back_matrix(second), preferred_element_type=jnp.float32)
    first_error = (back_one * slope_one).astype(jnp.bfloat16)
    grad_one = jnp.dot(first_layer_weights.T, first_error, preferred_element_type=jnp.float32) * grad_scale
    first_reach = jnp.concatenate((forward_shifted(first_error, DILATION_FIRST), first_error, backward_shifted(first_error, DILATION_FIRST)), 1)
    input_grad = (back_one + jnp.dot(first_reach, back_matrix(first), preferred_element_type=jnp.float32)).astype(jnp.bfloat16)
    return (input_grad, jnp.concatenate((grad_one, grad_two), 0))
```

```python
import functools
import math

import jax
import jax.numpy as jnp
from jax import lax
from jax.experimental import pallas as pl
from jax.experimental.pallas import tpu as pltpu
from jax.sharding import PartitionSpec as P

DILATION_FIRST = 1024
DILATION_SECOND = 2048
MESH = pl.DeviceIdType.MESH
CORES = 2
CHUNKS = 2
PAD = 16


def gelu_pair(pre_act):
    coeff = 0.7978845608
    tanh_value = jnp.tanh(coeff * (pre_act + 0.044715 * pre_act * pre_act * pre_act))
    gelu_value = 0.5 * pre_act * (1.0 + tanh_value)
    gelu_slope = 0.5 * (1.0 + tanh_value) + 0.5 * pre_act * (
        1.0 - tanh_value * tanh_value
    ) * coeff * (1.0 + 3.0 * 0.044715 * pre_act * pre_act)
    return (gelu_value, gelu_slope)


def kernel(
    groups, Z, S, fused, act, cot, wts, out, wg,
    A, CT, H, D2, D1, SL, B1, OG, W, WT, G, SB, RB, PB, RP, FB, OB, ssem, rsem,
):
    n, C = act.shape
    K = 3 * C
    X = S // CORES
    m = n // S
    mp = m // CHUNKS
    rows = n // CHUNKS
    tile = min(256, rows)
    y, z, s = lax.axis_index("grp"), lax.axis_index("seq"), lax.axis_index("sub")
    x, c = s // CORES, s % CORES
    other = 1 - c
    grad_scale = 1.0 / math.sqrt(n * S * Z)
    f32, bf16 = jnp.float32, jnp.bfloat16

    slots = {}

    def copy(name, src, dst, where):
        i = slots.setdefault(name, len(slots))
        return pltpu.make_async_remote_copy(
            src_ref=src, dst_ref=dst, send_sem=ssem.at[i], recv_sem=rsem.at[i],
            device_id=where, device_id_type=MESH,
        )

    def span(start, size):
        return pl.ds(pl.multiple_of(start, 16), size)

    pending = []

    barrier = pltpu.get_barrier_semaphore()
    greeted = 0

    def greet(where):
        pl.semaphore_signal(barrier, inc=1, device_id=where, device_id_type=MESH)

    for j in range(1, S):
        greet((y, z, (s + j) % S))
        greeted += 1
    for j in range(1, Z):
        for i in range(X) if fused else range(1):
            greet((y, (z + j) % Z, ((x + i) % X) * CORES + c))
            greeted += 1
    greet((1 - y, z, s))
    greeted += 1
    pl.semaphore_wait(barrier, greeted)

    w = wts.shape[0]
    hw = w // 2
    partner = (y, z, x * CORES + other)

    def half(shard, which):
        return W.at[span((shard * 2 + which) * hw, hw)]

    W[span(s * w, w), :] = wts[...]
    for j in range(1, X):
        d = copy(("wx", j), wts.at[span(y * hw, hw)], half(s, y), (y, z, ((x + j) % X) * CORES + c))
        d.start()
        pending.append(d)
    d = copy("wc", wts, W.at[span(s * w, w)], partner)
    d.start()
    pending.append(d)

    def spread(kind, source, target, lead, p):
        found = []
        for j in range(1, S):
            to = (s + j) % S
            d = copy(
                (kind, p, j), source.at[span(to * m + p * mp, mp)],
                target.at[p, span((lead + s) * mp, mp)], (y, z, to),
            )
            d.start()
            pending.append(d)
            found.append(d)
        target[p, span((lead + s) * mp, mp), :] = source[span(s * m + p * mp, mp), :]
        return found

    acts = [spread("a", act, A, 1, p) for p in range(CHUNKS)]

    def edges(buf, width):
        size = width * mp

        @pl.when(z == 0)
        def _():
            for p in range(CHUNKS):
                buf[p, 0:size, :] = jnp.zeros((size, C), bf16)

        @pl.when(z == Z - 1)
        def _():
            for p in range(CHUNKS):
                buf[p, size + rows : 2 * size + rows, :] = jnp.zeros((size, C), bf16)

    edges(A, 1)
    edges(H, 2)
    edges(D2, 2)
    edges(D1, 1)
    if fused:
        PB[...] = jnp.zeros(PB.shape, bf16)

    halos = []

    def halo_pair(kind, buf, width, p):
        size = width * mp
        up = copy(
            (kind, "up", p), buf.at[p, pl.ds(rows, size)], buf.at[p, pl.ds(0, size)],
            (y, jnp.minimum(z + 1, Z - 1), s),
        )
        down = copy(
            (kind, "down", p), buf.at[p, pl.ds(size, size)], buf.at[p, pl.ds(size + rows, size)],
            (y, jnp.maximum(z - 1, 0), s),
        )
        return up, down

    def halo_send(kind, buf, width, p):
        up, down = halo_pair(kind, buf, width, p)

        @pl.when(z < Z - 1)
        def _():
            up.start()

        @pl.when(z > 0)
        def _():
            down.start()

        halos.append((kind, buf, width, p))

    def halo_wait(kind, buf, width, p):
        up, down = halo_pair(kind, buf, width, p)

        @pl.when(z > 0)
        def _():
            up.wait_recv()

        @pl.when(z < Z - 1)
        def _():
            down.wait_recv()

    forwards = []
    for j in range(1, X):
        source = ((x + X - j) % X) * CORES + c
        copy(("wx", j), half(source, y), half(source, y), partner).wait_recv()
        d = copy(("wy", j), half(source, y), half(source, y), (1 - y, z, s))
        d.start()
        pending.append(d)
        d = copy(("wca", j), half(source, y), half(source, y), partner)
        d.start()
        pending.append(d)
    for j in range(1, X):
        source = ((x + X - j) % X) * CORES + c
        theirs = half(source, 1 - y)
        copy(("wy", j), theirs, theirs, partner).wait_recv()
        d = copy(("wcb", j), theirs, theirs, partner)
        d.start()
        pending.append(d)

    for p in range(CHUNKS):
        for d in acts[p]:
            d.wait_recv()
        halo_send("ha", A, 1, p)
    cots = [spread("c", cot, CT, 0, p) for p in range(CHUNKS)]

    pending[X - 1].wait_recv()
    for j in range(1, X):
        source = ((x + X - j) % X) * CORES + other
        copy(("wca", j), half(source, y), half(source, y), partner).wait_recv()
        copy(("wcb", j), half(source, 1 - y), half(source, 1 - y), partner).wait_recv()
    for k in range(6):
        WT[k * C : (k + 1) * C, :] = W[k * C : (k + 1) * C, :].T

    def three(buf, p, width, start, back):
        taps = [buf[p, span(start + k * width * mp, tile), :] for k in range(3)]
        return jnp.concatenate(taps[::-1] if back else taps, 1)

    def tiles(body):
        def step(t, carry):
            body(t * tile)
            return carry

        lax.fori_loop(0, rows // tile, step, 0)

    for p in range(CHUNKS):
        halo_wait("ha", A, 1, p)

        def layer_one(start):
            pre = jnp.dot(three(A, p, 1, start, False), W[0:K, :], preferred_element_type=f32)
            value, slope = gelu_pair(pre)
            SL[p, span(start, tile), :] = slope
            own = A[p, span(start + mp, tile), :].astype(f32)
            H[p, span(start + 2 * mp, tile), :] = (own + value).astype(bf16)

        tiles(layer_one)
        halo_send("hh", H, 2, p)

    for p in range(CHUNKS):
        for d in cots[p]:
            d.wait_recv()
        halo_wait("hh", H, 2, p)

        def layer_two(start):
            pre = jnp.dot(three(H, p, 2, start, False), W[K : 2 * K, :], preferred_element_type=f32)
            slope = gelu_pair(pre)[1]
            here = CT[p, span(start, tile), :].astype(f32)
            D2[p, span(start + 2 * mp, tile), :] = (here * slope).astype(bf16)

        tiles(layer_two)
        halo_send("hd", D2, 2, p)

    def grads(layer, buf, width, delta):
        for k in range(3):
            total = None
            for p in range(CHUNKS):
                part = lax.dot_general(
                    buf[p, k * width * mp : k * width * mp + rows, :],
                    delta[p, width * mp : width * mp + rows, :],
                    (((0,), (0,)), ((), ())), preferred_element_type=f32,
                )
                total = part if total is None else total + part
            G[layer, k * C : (k + 1) * C, :] = total

    hk = K // 2
    ring = Z * X
    me = z * X + x
    piece = hk // ring

    def pair_send(layer):
        SB[layer, :, :] = G[layer, span(other * hk, hk), :].astype(bf16)
        d = copy(("pair", layer), SB.at[layer], RB.at[layer], partner)
        d.start()
        pending.append(d)
        return d

    def scatter(layer, d):
        d.wait_recv()
        found = []
        for k in range(ring):
            mine = G[layer, pl.ds(pl.multiple_of(c * hk + k * piece, 8), piece), :]
            PB[layer, k, 0:piece, :] = (
                mine + RB[layer, k * piece : (k + 1) * piece, :].astype(f32)
            ).astype(bf16)
        for j in range(1, ring):
            to = (me + j) % ring
            d = copy(
                ("rs", layer, j), PB.at[layer, to], RP.at[layer, j - 1],
                (y, to // X, (to % X) * CORES + c),
            )
            d.start()
            pending.append(d)
            found.append(d)
        return found

    gathers = []

    def gather_copy(layer, xs, dz):
        return copy(
            ("ag", xs, dz), FB.at[layer], OB.at[me], (y, (z + dz) % Z, layer * CORES + c)
        )

    def gather(layer, found):
        total = PB[layer, me].astype(f32)
        for j, d in enumerate(found):
            d.wait_recv()
            total = total + RP[layer, j].astype(f32)
        FB[layer] = (total * grad_scale).astype(bf16)
        for xs in range(X):

            @pl.when(x == xs)
            def _():
                for dz in range(Z):
                    if xs == layer and dz == 0:
                        OB[me] = FB[layer]
                    else:
                        gather_copy(layer, xs, dz).start()

            gathers.append((layer, xs))

    grads(1, H, 2, D2)
    if fused:
        pair_two = pair_send(1)

    for p in range(CHUNKS):
        halo_wait("hd", D2, 2, p)

        def back_two(start):
            total = CT[p, span(start, tile), :].astype(f32) + jnp.dot(
                three(D2, p, 2, start, True), WT[K : 2 * K, :], preferred_element_type=f32
            )
            B1[p, span(start, tile), :] = total
            D1[p, span(start + mp, tile), :] = (total * SL[p, span(start, tile), :]).astype(bf16)

        tiles(back_two)
        halo_send("he", D1, 1, p)

    if fused:
        found_two = scatter(1, pair_two)
    grads(0, A, 1, D1)
    if fused:
        pair_one = pair_send(0)

    for p in range(CHUNKS):
        halo_wait("he", D1, 1, p)

        def back_one(start):
            OG[p, span(start, tile), :] = (
                B1[p, span(start, tile), :]
                + jnp.dot(three(D1, p, 1, start, True), WT[0:K, :], preferred_element_type=f32)
            ).astype(bf16)

        tiles(back_one)
        if fused and p == 0:
            found_one = scatter(0, pair_one)
        for j in range(1, S):
            to = (s + j) % S
            d = copy(
                ("o", p, j), OG.at[p, span(to * mp, mp)], out.at[span(s * m + p * mp, mp)],
                (y, z, to),
            )
            d.start()
            pending.append(d)
        out[span(s * m + p * mp, mp), :] = OG[p, span(s * mp, mp), :]

    if fused:
        gather(1, found_two)
        gather(0, found_one)
        for layer in range(2):

            @pl.when(x == layer)
            def _():
                for xs in range(X):
                    for dz in range(Z):
                        if xs != layer or dz != 0:
                            gather_copy(layer, xs, dz).wait_recv()
                for k in range(ring):
                    wg[k * piece : (k + 1) * piece, :] = OB[k, 0:piece, :].astype(f32)
    else:
        wg[...] = G[...].reshape(2 * K, C)

    for p in range(CHUNKS):
        for j in range(1, S):
            came = out.at[span(((s + S - j) % S) * m + p * mp, mp)]
            copy(("o", p, j), came, came, partner).wait_recv()
    for d in pending:
        d.wait_send()
    for kind, buf, width, p in halos:
        up, down = halo_pair(kind, buf, width, p)
        pl.when(z < Z - 1)(up.wait_send)
        pl.when(z > 0)(down.wait_send)
    for layer, xs in gathers:

        @pl.when(x == xs)
        def _():
            for dz in range(Z):
                if xs != layer or dz != 0:
                    gather_copy(layer, xs, dz).wait_send()


def per_device(groups, Z, S, activations, cotangent, weights):
    n, C = activations.shape
    assert n == DILATION_FIRST and 2 * n == DILATION_SECOND and groups == 2 and S >= 2 * CORES
    K = 3 * C
    X = S // CORES
    ring = Z * X
    mp = n // S // CHUNKS
    rows = n // CHUNKS
    fused = X == 2 and (K // 2) % (8 * ring) == 0
    piece = K // 2 // ring if fused else PAD
    padded = -(-piece // PAD) * PAD
    pieces = ring if fused else 2
    hk = K // 2 if fused else PAD
    bf16, f32 = jnp.bfloat16, jnp.float32
    semaphores = (S - 1) * CHUNKS * 3 + 8 * CHUNKS + 1 + 4 * X + 2 * (1 + ring) + ring + 8
    vmem = pl.BlockSpec(memory_space=pltpu.VMEM)
    input_grad, grads = pl.pallas_call(
        functools.partial(kernel, groups, Z, S, fused),
        out_shape=(
            jax.ShapeDtypeStruct((n, C), bf16),
            jax.ShapeDtypeStruct((weights.shape[0] if fused else 2 * K, C), f32),
        ),
        in_specs=[vmem] * 3,
        out_specs=(vmem, vmem),
        scratch_shapes=[
            pltpu.VMEM((CHUNKS, rows + 2 * mp, C), bf16),
            pltpu.VMEM((CHUNKS, rows, C), bf16),
            pltpu.VMEM((CHUNKS, rows + 4 * mp, C), bf16),
            pltpu.VMEM((CHUNKS, rows + 4 * mp, C), bf16),
            pltpu.VMEM((CHUNKS, rows + 2 * mp, C), bf16),
            pltpu.VMEM((CHUNKS, rows, C), f32),
            pltpu.VMEM((CHUNKS, rows, C), f32),
            pltpu.VMEM((CHUNKS, rows, C), bf16),
            pltpu.VMEM((2 * K, C), bf16),
            pltpu.VMEM((2 * K, C), bf16),
            pltpu.VMEM((2, K, C), f32),
            pltpu.VMEM((2, hk, C), bf16),
            pltpu.VMEM((2, hk, C), bf16),
            pltpu.VMEM((2, pieces, padded, C), bf16),
            pltpu.VMEM((2, pieces - 1, padded, C), bf16),
            pltpu.VMEM((2, padded, C), bf16),
            pltpu.VMEM((pieces, padded, C), bf16),
            pltpu.SemaphoreType.DMA((semaphores,)),
            pltpu.SemaphoreType.DMA((semaphores,)),
        ],
        compiler_params=pltpu.CompilerParams(
            collective_id=0, has_side_effects=True, vmem_limit_bytes=48 * 1024 * 1024
        ),
        name="layers_backward",
    )(activations, cotangent, weights)
    if not fused:
        scale = 1.0 / math.sqrt(n * S * Z)
        grads = lax.psum(grads * scale, "seq")
        grads = lax.psum_scatter(grads, "sub", scatter_dimension=0, tiled=True)
    return (input_grad, grads)


def solution(mesh):
    placed = (P(("grp", "seq", "sub"), None), P(("grp", "seq", "sub"), None), P("sub", None))
    sizes = [mesh.shape[axis] for axis in ("grp", "seq", "sub")]
    return jax.shard_map(
        functools.partial(per_device, *sizes),
        mesh=mesh,
        in_specs=placed,
        out_specs=(P(("grp", "seq", "sub"), None), P(("grp", "sub"), None)),
        check_vma=False,
    )
```

```python
import functools
import math

import jax
import jax.numpy as jnp
from jax import lax
from jax.experimental import pallas as pl
from jax.experimental.pallas import tpu as pltpu
from jax.sharding import PartitionSpec as P

DILATION_FIRST = 1024
DILATION_SECOND = 2048
MESH = pl.DeviceIdType.MESH
CORES = 2
CHUNKS = 2
PAD = 16


def gelu_pair(pre_act):
    coeff = 0.7978845608
    tanh_value = jnp.tanh(coeff * (pre_act + 0.044715 * pre_act * pre_act * pre_act))
    gelu_value = 0.5 * pre_act * (1.0 + tanh_value)
    gelu_slope = 0.5 * (1.0 + tanh_value) + 0.5 * pre_act * (
        1.0 - tanh_value * tanh_value
    ) * coeff * (1.0 + 3.0 * 0.044715 * pre_act * pre_act)
    return (gelu_value, gelu_slope)


def kernel(
    groups, Z, S, fused, act, cot, wts, out, wg,
    A, CT, H, D2, D1, SL, B1, OG, W, WT, G, SB, RB, XB, XR, PB, RP, FB, OB, ssem, rsem, lsem,
):
    n, C = act.shape
    K = 3 * C
    X = S // CORES
    m = n // S
    mp = m // CHUNKS
    rows = n // CHUNKS
    tile = min(256, rows)
    y, z, s = lax.axis_index("grp"), lax.axis_index("seq"), lax.axis_index("sub")
    x, c = s // CORES, s % CORES
    other = 1 - c
    grad_scale = 1.0 / math.sqrt(n * S * Z)
    f32, bf16 = jnp.float32, jnp.bfloat16

    slots = {}

    def copy(name, src, dst, where):
        i = slots.setdefault(name, len(slots))
        return pltpu.make_async_remote_copy(
            src_ref=src, dst_ref=dst, send_sem=ssem.at[i], recv_sem=rsem.at[i],
            device_id=where, device_id_type=MESH,
        )

    def span(start, size):
        return pl.ds(pl.multiple_of(start, 16), size)

    pending = []
    local = {}

    def bring(name, src, dst):
        local[name] = pltpu.make_async_copy(src, dst, lsem.at[len(local)])
        local[name].start()

    barrier = pltpu.get_barrier_semaphore()
    greeted = 0

    def greet(where):
        pl.semaphore_signal(barrier, inc=1, device_id=where, device_id_type=MESH)

    for j in range(1, S):
        greet((y, z, (s + j) % S))
        greeted += 1
    for j in range(1, Z):
        greet((y, (z + j) % Z, s))
        greeted += 1
    greet((1 - y, z, s))
    greeted += 1
    pl.semaphore_wait(barrier, greeted)

    w = wts.shape[0]
    hw = w // 2
    partner = (y, z, x * CORES + other)

    def half(shard, which):
        return W.at[span((shard * 2 + which) * hw, hw)]

    for j in range(1, X):
        d = copy(("wx", j), wts.at[span(y * hw, hw)], half(s, y), (y, z, ((x + j) % X) * CORES + c))
        d.start()
        pending.append(d)
    d = copy("wc", wts, W.at[span(s * w, w)], partner)
    d.start()
    pending.append(d)

    def spread(kind, source, target, lead, p):
        found = []
        for j in range(1, S):
            to = (s + j) % S
            d = copy(
                (kind, p, j), source.at[span(to * m + p * mp, mp)],
                target.at[p, span((lead + s) * mp, mp)], (y, z, to),
            )
            d.start()
            pending.append(d)
            found.append(d)
        bring(
            (kind, p), source.at[span(s * m + p * mp, mp)],
            target.at[p, span((lead + s) * mp, mp)],
        )
        return found

    acts = [spread("a", act, A, 1, p) for p in range(CHUNKS)]
    bring("w", wts, W.at[span(s * w, w)])

    def edges(buf, width):
        size = width * mp

        @pl.when(z == 0)
        def _():
            for p in range(CHUNKS):
                buf[p, 0:size, :] = jnp.zeros((size, C), bf16)

        @pl.when(z == Z - 1)
        def _():
            for p in range(CHUNKS):
                buf[p, size + rows : 2 * size + rows, :] = jnp.zeros((size, C), bf16)

    edges(A, 1)
    edges(H, 2)
    edges(D2, 2)
    edges(D1, 1)
    if fused:
        PB[...] = jnp.zeros(PB.shape, bf16)

    halos = []

    def halo_pair(kind, buf, width, p):
        size = width * mp
        up = copy(
            (kind, "up", p), buf.at[p, pl.ds(rows, size)], buf.at[p, pl.ds(0, size)],
            (y, jnp.minimum(z + 1, Z - 1), s),
        )
        down = copy(
            (kind, "down", p), buf.at[p, pl.ds(size, size)], buf.at[p, pl.ds(size + rows, size)],
            (y, jnp.maximum(z - 1, 0), s),
        )
        return up, down

    def halo_send(kind, buf, width, p):
        up, down = halo_pair(kind, buf, width, p)

        @pl.when(z < Z - 1)
        def _():
            up.start()

        @pl.when(z > 0)
        def _():
            down.start()

        halos.append((kind, buf, width, p))

    def halo_wait(kind, buf, width, p):
        up, down = halo_pair(kind, buf, width, p)

        @pl.when(z > 0)
        def _():
            up.wait_recv()

        @pl.when(z < Z - 1)
        def _():
            down.wait_recv()

    forwards = []
    for j in range(1, X):
        source = ((x + X - j) % X) * CORES + c
        copy(("wx", j), half(source, y), half(source, y), partner).wait_recv()
        d = copy(("wy", j), half(source, y), half(source, y), (1 - y, z, s))
        d.start()
        pending.append(d)
        d = copy(("wca", j), half(source, y), half(source, y), partner)
        d.start()
        pending.append(d)
    for j in range(1, X):
        source = ((x + X - j) % X) * CORES + c
        theirs = half(source, 1 - y)
        copy(("wy", j), theirs, theirs, partner).wait_recv()
        d = copy(("wcb", j), theirs, theirs, partner)
        d.start()
        pending.append(d)

    for p in range(CHUNKS):
        local["a", p].wait()
        for d in acts[p]:
            d.wait_recv()
        halo_send("ha", A, 1, p)
    cots = [spread("c", cot, CT, 0, p) for p in range(CHUNKS)]

    local["w"].wait()
    pending[X - 1].wait_recv()
    for j in range(1, X):
        source = ((x + X - j) % X) * CORES + other
        copy(("wca", j), half(source, y), half(source, y), partner).wait_recv()
        copy(("wcb", j), half(source, 1 - y), half(source, 1 - y), partner).wait_recv()

    def three(buf, p, width, start, back):
        taps = [buf[p, span(start + k * width * mp, tile), :] for k in range(3)]
        return jnp.concatenate(taps[::-1] if back else taps, 1)

    def tiles(body):
        def step(t, carry):
            body(t * tile)
            return carry

        lax.fori_loop(0, rows // tile, step, 0)

    for p in range(CHUNKS):
        halo_wait("ha", A, 1, p)

        def layer_one(start):
            pre = jnp.dot(three(A, p, 1, start, False), W[0:K, :], preferred_element_type=f32)
            value, slope = gelu_pair(pre)
            SL[p, span(start, tile), :] = slope
            own = A[p, span(start + mp, tile), :].astype(f32)
            H[p, span(start + 2 * mp, tile), :] = (own + value).astype(bf16)

        tiles(layer_one)
        halo_send("hh", H, 2, p)

    for k in range(6):
        WT[k * C : (k + 1) * C, :] = W[k * C : (k + 1) * C, :].T

    for p in range(CHUNKS):
        local["c", p].wait()
        for d in cots[p]:
            d.wait_recv()
        halo_wait("hh", H, 2, p)

        def layer_two(start):
            pre = jnp.dot(three(H, p, 2, start, False), W[K : 2 * K, :], preferred_element_type=f32)
            slope = gelu_pair(pre)[1]
            here = CT[p, span(start, tile), :].astype(f32)
            D2[p, span(start + 2 * mp, tile), :] = (here * slope).astype(bf16)

        tiles(layer_two)
        halo_send("hd", D2, 2, p)

    def grads(layer, buf, width, delta):
        for k in range(3):
            total = None
            for p in range(CHUNKS):
                part = lax.dot_general(
                    buf[p, k * width * mp : k * width * mp + rows, :],
                    delta[p, width * mp : width * mp + rows, :],
                    (((0,), (0,)), ((), ())), preferred_element_type=f32,
                )
                total = part if total is None else total + part
            G[layer, k * C : (k + 1) * C, :] = total

    hk = K // 2
    qk = hk // 2
    piece = qk // Z

    def pair_send(layer):
        SB[layer, :, :] = G[layer, span(other * hk, hk), :].astype(bf16)
        d = copy(("pair", layer), SB.at[layer], RB.at[layer], partner)
        d.start()
        pending.append(d)
        return d

    def across_x(layer, d):
        d.wait_recv()
        there = (1 - x) * qk
        XB[layer] = (
            G[layer, span(c * hk + there, qk), :] + RB[layer, span(there, qk), :].astype(f32)
        ).astype(bf16)
        d = copy(("x", layer), XB.at[layer], XR.at[layer], (y, z, (1 - x) * CORES + c))
        d.start()
        pending.append(d)
        return d

    def scatter(layer, d):
        here = x * qk
        both = G[layer, span(c * hk + here, qk), :] + RB[layer, span(here, qk), :].astype(f32)
        d.wait_recv()
        both = (both + XR[layer].astype(f32)).astype(bf16)
        for k in range(Z):
            PB[layer, k, 0:piece, :] = both[k * piece : (k + 1) * piece, :]
        found = []
        for j in range(1, Z):
            to = (z + j) % Z
            d = copy(("rs", layer, j), PB.at[layer, to], RP.at[layer, j - 1], (y, to, s))
            d.start()
            pending.append(d)
            found.append(d)
        return found

    def give(layer):
        at = OB.at[1 - layer, z]
        return copy("give", FB.at[layer], at, (y, z, layer * CORES + c))

    def along_z(which, dz):
        at = OB.at[which, z]
        return copy(("ag", which, dz), at, at, (y, (z + dz) % Z, s))

    def gather(layer, found):
        total = PB[layer, z].astype(f32)
        for j, d in enumerate(found):
            d.wait_recv()
            total = total + RP[layer, j].astype(f32)
        result = (total * grad_scale).astype(bf16)

        @pl.when(x == layer)
        def _():
            OB[layer, z] = result
            for dz in range(1, Z):
                along_z(layer, dz).start()

        @pl.when(x != layer)
        def _():
            FB[layer] = result
            give(layer).start()

    def pass_on(layer):
        @pl.when(x == layer)
        def _():
            give(layer).wait_recv()
            for dz in range(1, Z):
                along_z(1 - layer, dz).start()

    def collect(layer):
        @pl.when(x == layer)
        def _():
            for which in range(2):
                for dz in range(1, Z):
                    along_z(which, dz).wait_recv()
            for which in range(2):
                for k in range(Z):
                    row = which * qk + k * piece
                    wg[row : row + piece, :] = OB[which, k, 0:piece, :].astype(f32)
            for which in range(2):
                for dz in range(1, Z):
                    along_z(which, dz).wait_send()

        pl.when(x != layer)(give(layer).wait_send)

    grads(1, H, 2, D2)
    if fused:
        pair_two = pair_send(1)

    for p in range(CHUNKS):
        halo_wait("hd", D2, 2, p)

        def back_two(start):
            total = CT[p, span(start, tile), :].astype(f32) + jnp.dot(
                three(D2, p, 2, start, True), WT[K : 2 * K, :], preferred_element_type=f32
            )
            B1[p, span(start, tile), :] = total
            D1[p, span(start + mp, tile), :] = (total * SL[p, span(start, tile), :]).astype(bf16)

        tiles(back_two)
        halo_send("he", D1, 1, p)

    if fused:
        cross_two = across_x(1, pair_two)
    grads(0, A, 1, D1)
    if fused:
        pair_one = pair_send(0)
        found_two = scatter(1, cross_two)
        cross_one = across_x(0, pair_one)

    for p in range(CHUNKS):
        halo_wait("he", D1, 1, p)

        def back_one(start):
            OG[p, span(start, tile), :] = (
                B1[p, span(start, tile), :]
                + jnp.dot(three(D1, p, 1, start, True), WT[0:K, :], preferred_element_type=f32)
            ).astype(bf16)

        tiles(back_one)
        if fused and p == 0:
            found_one = scatter(0, cross_one)
        for j in range(1, S):
            to = (s + j) % S
            d = copy(
                ("o", p, j), OG.at[p, span(to * mp, mp)], out.at[span(s * m + p * mp, mp)],
                (y, z, to),
            )
            d.start()
            pending.append(d)
        out[span(s * m + p * mp, mp), :] = OG[p, span(s * mp, mp), :]

    if fused:
        gather(1, found_two)
        gather(0, found_one)
        pass_on(1)
        pass_on(0)
        collect(1)
        collect(0)
    else:
        wg[...] = G[...].reshape(2 * K, C)

    for p in range(CHUNKS):
        for j in range(1, S):
            came = out.at[span(((s + S - j) % S) * m + p * mp, mp)]
            copy(("o", p, j), came, came, partner).wait_recv()
    for d in pending:
        d.wait_send()
    for kind, buf, width, p in halos:
        up, down = halo_pair(kind, buf, width, p)
        pl.when(z < Z - 1)(up.wait_send)
        pl.when(z > 0)(down.wait_send)


def per_device(groups, Z, S, activations, cotangent, weights):
    n, C = activations.shape
    assert n == DILATION_FIRST and 2 * n == DILATION_SECOND and groups == 2 and S >= 2 * CORES
    K = 3 * C
    X = S // CORES
    mp = n // S // CHUNKS
    rows = n // CHUNKS
    fused = X == 2 and (K // 4) % (8 * Z) == 0 and (K // 4) % PAD == 0
    piece = K // 4 // Z if fused else PAD
    padded = -(-piece // PAD) * PAD
    pieces = Z if fused else 2
    qk = K // 4 if fused else PAD
    hk = K // 2 if fused else PAD
    bf16, f32 = jnp.bfloat16, jnp.float32
    semaphores = (S - 1) * CHUNKS * 3 + 8 * CHUNKS + 1 + 4 * X + 2 * (2 + Z) + 1 + 2 * Z + 8
    vmem = pl.BlockSpec(memory_space=pltpu.VMEM)
    input_grad, grads = pl.pallas_call(
        functools.partial(kernel, groups, Z, S, fused),
        out_shape=(
            jax.ShapeDtypeStruct((n, C), bf16),
            jax.ShapeDtypeStruct((weights.shape[0] if fused else 2 * K, C), f32),
        ),
        in_specs=[pl.BlockSpec(memory_space=pltpu.HBM)] * 3,
        out_specs=(vmem, vmem),
        scratch_shapes=[
            pltpu.VMEM((CHUNKS, rows + 2 * mp, C), bf16),
            pltpu.VMEM((CHUNKS, rows, C), bf16),
            pltpu.VMEM((CHUNKS, rows + 4 * mp, C), bf16),
            pltpu.VMEM((CHUNKS, rows + 4 * mp, C), bf16),
            pltpu.VMEM((CHUNKS, rows + 2 * mp, C), bf16),
            pltpu.VMEM((CHUNKS, rows, C), f32),
            pltpu.VMEM((CHUNKS, rows, C), f32),
            pltpu.VMEM((CHUNKS, rows, C), bf16),
            pltpu.VMEM((2 * K, C), bf16),
            pltpu.VMEM((2 * K, C), bf16),
            pltpu.VMEM((2, K, C), f32),
            pltpu.VMEM((2, hk, C), bf16),
            pltpu.VMEM((2, hk, C), bf16),
            pltpu.VMEM((2, qk, C), bf16),
            pltpu.VMEM((2, qk, C), bf16),
            pltpu.VMEM((2, pieces, padded, C), bf16),
            pltpu.VMEM((2, pieces - 1, padded, C), bf16),
            pltpu.VMEM((2, padded, C), bf16),
            pltpu.VMEM((2, pieces, padded, C), bf16),
            pltpu.SemaphoreType.DMA((semaphores,)),
            pltpu.SemaphoreType.DMA((semaphores,)),
            pltpu.SemaphoreType.DMA((2 * CHUNKS + 1,)),
        ],
        compiler_params=pltpu.CompilerParams(
            collective_id=0, has_side_effects=True, vmem_limit_bytes=48 * 1024 * 1024
        ),
        name="layers_backward",
    )(activations, cotangent, weights)
    if not fused:
        scale = 1.0 / math.sqrt(n * S * Z)
        grads = lax.psum(grads * scale, "seq")
        grads = lax.psum_scatter(grads, "sub", scatter_dimension=0, tiled=True)
    return (input_grad, grads)


def solution(mesh):
    placed = (P(("grp", "seq", "sub"), None), P(("grp", "seq", "sub"), None), P("sub", None))
    sizes = [mesh.shape[axis] for axis in ("grp", "seq", "sub")]
    return jax.shard_map(
        functools.partial(per_device, *sizes),
        mesh=mesh,
        in_specs=placed,
        out_specs=(P(("grp", "seq", "sub"), None), P(("grp", "sub"), None)),
        check_vma=False,
    )
```

```python
import functools
import math

import jax
import jax.numpy as jnp
from jax import lax
from jax.experimental import pallas as pl
from jax.experimental.pallas import tpu as pltpu
from jax.sharding import PartitionSpec as P

DILATION_FIRST = 1024
DILATION_SECOND = 2048
MESH = pl.DeviceIdType.MESH
CORES = 2
CHUNKS = 2
PAD = 16


def gelu_pair(pre_act):
    coeff = 0.7978845608
    tanh_value = jnp.tanh(coeff * (pre_act + 0.044715 * pre_act * pre_act * pre_act))
    gelu_value = 0.5 * pre_act * (1.0 + tanh_value)
    gelu_slope = 0.5 * (1.0 + tanh_value) + 0.5 * pre_act * (
        1.0 - tanh_value * tanh_value
    ) * coeff * (1.0 + 3.0 * 0.044715 * pre_act * pre_act)
    return (gelu_value, gelu_slope)


def kernel(
    groups, Z, S, fused, act, cot, wts, out, wg,
    A, CT, H, D2, D1, SL, B1, OG, W, WT, G, SB, RB, XB, XR, PB, RP, FB, OB, ssem, rsem, lsem,
):
    n, C = act.shape
    K = 3 * C
    X = S // CORES
    m = n // S
    mp = m // CHUNKS
    rows = n // CHUNKS
    tile = min(256, rows)
    y, z, s = lax.axis_index("grp"), lax.axis_index("seq"), lax.axis_index("sub")
    x, c = s // CORES, s % CORES
    other = 1 - c
    grad_scale = 1.0 / math.sqrt(n * S * Z)
    f32, bf16 = jnp.float32, jnp.bfloat16

    slots = {}

    def copy(name, src, dst, where):
        i = slots.setdefault(name, len(slots))
        return pltpu.make_async_remote_copy(
            src_ref=src, dst_ref=dst, send_sem=ssem.at[i], recv_sem=rsem.at[i],
            device_id=where, device_id_type=MESH,
        )

    def span(start, size):
        return pl.ds(pl.multiple_of(start, 16), size)

    pending = []
    local = {}

    def bring(name, src, dst):
        local[name] = pltpu.make_async_copy(src, dst, lsem.at[len(local)])
        local[name].start()

    barrier = pltpu.get_barrier_semaphore()
    greeted = 0

    def greet(where):
        pl.semaphore_signal(barrier, inc=1, device_id=where, device_id_type=MESH)

    for j in range(1, S):
        greet((y, z, (s + j) % S))
        greeted += 1
    for j in range(1, Z):
        greet((y, (z + j) % Z, s))
        greeted += 1
    greet((1 - y, z, s))
    greeted += 1
    pl.semaphore_wait(barrier, greeted)

    w = wts.shape[0]
    zs = 2 if Z % 2 == 0 and w % (4 * PAD) == 0 else 1
    pw = w // (2 * zs)
    h = z % zs
    partner = (y, z, x * CORES + other)
    beside = (y, z + 1 - 2 * h, s)
    across = (1 - y, z, s)

    def piece_of(shard, group, which):
        return W.at[span(shard * w + (group * zs + which) * pw, pw)]

    for j in range(1, X):
        d = copy(
            ("wx", j), wts.at[span((y * zs + h) * pw, pw)], piece_of(s, y, h),
            (y, z, ((x + j) % X) * CORES + c),
        )
        d.start()
        pending.append(d)
    d = copy("wc", wts, W.at[span(s * w, w)], partner)
    d.start()
    pending.append(d)

    def spread(kind, source, target, lead, p):
        found = []
        for j in range(1, S):
            to = (s + j) % S
            d = copy(
                (kind, p, j), source.at[span(to * m + p * mp, mp)],
                target.at[p, span((lead + s) * mp, mp)], (y, z, to),
            )
            d.start()
            pending.append(d)
            found.append(d)
        bring(
            (kind, p), source.at[span(s * m + p * mp, mp)],
            target.at[p, span((lead + s) * mp, mp)],
        )
        return found

    acts = [spread("a", act, A, 1, p) for p in range(CHUNKS)]
    bring("w", wts, W.at[span(s * w, w)])

    def edges(buf, width):
        size = width * mp

        @pl.when(z == 0)
        def _():
            for p in range(CHUNKS):
                buf[p, 0:size, :] = jnp.zeros((size, C), bf16)

        @pl.when(z == Z - 1)
        def _():
            for p in range(CHUNKS):
                buf[p, size + rows : 2 * size + rows, :] = jnp.zeros((size, C), bf16)

    edges(A, 1)
    edges(H, 2)
    edges(D2, 2)
    edges(D1, 1)
    if fused:
        PB[...] = jnp.zeros(PB.shape, bf16)

    halos = []

    def halo_pair(kind, buf, width, p):
        size = width * mp
        up = copy(
            (kind, "up", p), buf.at[p, pl.ds(rows, size)], buf.at[p, pl.ds(0, size)],
            (y, jnp.minimum(z + 1, Z - 1), s),
        )
        down = copy(
            (kind, "down", p), buf.at[p, pl.ds(size, size)], buf.at[p, pl.ds(size + rows, size)],
            (y, jnp.maximum(z - 1, 0), s),
        )
        return up, down

    def halo_send(kind, buf, width, p):
        up, down = halo_pair(kind, buf, width, p)

        @pl.when(z < Z - 1)
        def _():
            up.start()

        @pl.when(z > 0)
        def _():
            down.start()

        halos.append((kind, buf, width, p))

    def halo_wait(kind, buf, width, p):
        up, down = halo_pair(kind, buf, width, p)

        @pl.when(z > 0)
        def _():
            up.wait_recv()

        @pl.when(z < Z - 1)
        def _():
            down.wait_recv()

    def forward(name, ref, where):
        d = copy(name, ref, ref, where)
        d.start()
        pending.append(d)

    def arrived(name, ref):
        copy(name, ref, ref, partner).wait_recv()

    for j in range(1, X):
        source = ((x + X - j) % X) * CORES + c
        mine = piece_of(source, y, h)
        arrived(("wx", j), mine)
        if zs == 2:
            forward(("wz", j), mine, beside)
        forward(("wy", j, 0), mine, across)
        forward(("wca", j, 0), mine, partner)
    for j in range(1, X) if zs == 2 else ():
        source = ((x + X - j) % X) * CORES + c
        theirs = piece_of(source, y, 1 - h)
        arrived(("wz", j), theirs)
        forward(("wy", j, 1), theirs, across)
        forward(("wca", j, 1), theirs, partner)
    for j in range(1, X):
        source = ((x + X - j) % X) * CORES + c
        for i in range(zs):
            theirs = piece_of(source, 1 - y, (h + i) % zs)
            arrived(("wy", j, i), theirs)
            forward(("wcb", j, i), theirs, partner)

    for p in range(CHUNKS):
        local["a", p].wait()
        for d in acts[p]:
            d.wait_recv()
        halo_send("ha", A, 1, p)
    cots = [spread("c", cot, CT, 0, p) for p in range(CHUNKS)]

    local["w"].wait()
    pending[X - 1].wait_recv()
    for j in range(1, X):
        source = ((x + X - j) % X) * CORES + other
        for i in range(zs):
            arrived(("wca", j, i), piece_of(source, y, (h + i) % zs))
            arrived(("wcb", j, i), piece_of(source, 1 - y, (h + i) % zs))

    def three(buf, p, width, start, back):
        taps = [buf[p, span(start + k * width * mp, tile), :] for k in range(3)]
        return jnp.concatenate(taps[::-1] if back else taps, 1)

    def tiles(body):
        def step(t, carry):
            body(t * tile)
            return carry

        lax.fori_loop(0, rows // tile, step, 0)

    for p in range(CHUNKS):
        halo_wait("ha", A, 1, p)

        def layer_one(start):
            pre = jnp.dot(three(A, p, 1, start, False), W[0:K, :], preferred_element_type=f32)
            value, slope = gelu_pair(pre)
            SL[p, span(start, tile), :] = slope
            own = A[p, span(start + mp, tile), :].astype(f32)
            H[p, span(start + 2 * mp, tile), :] = (own + value).astype(bf16)

        tiles(layer_one)
        halo_send("hh", H, 2, p)

    for k in range(6):
        WT[k * C : (k + 1) * C, :] = W[k * C : (k + 1) * C, :].T

    for p in range(CHUNKS):
        local["c", p].wait()
        for d in cots[p]:
            d.wait_recv()
        halo_wait("hh", H, 2, p)

        def layer_two(start):
            pre = jnp.dot(three(H, p, 2, start, False), W[K : 2 * K, :], preferred_element_type=f32)
            slope = gelu_pair(pre)[1]
            here = CT[p, span(start, tile), :].astype(f32)
            D2[p, span(start + 2 * mp, tile), :] = (here * slope).astype(bf16)

        tiles(layer_two)
        halo_send("hd", D2, 2, p)

    def grads(layer, buf, width, delta):
        right = jnp.concatenate(
            [delta[p, width * mp : width * mp + rows, :] for p in range(CHUNKS)], 0
        )
        for k in range(3):
            start = k * width * mp
            left = jnp.concatenate([buf[p, start : start + rows, :] for p in range(CHUNKS)], 0)
            G[layer, k * C : (k + 1) * C, :] = lax.dot_general(
                left, right, (((0,), (0,)), ((), ())), preferred_element_type=f32
            )

    hk = K // 2
    qk = hk // 2
    piece = qk // Z

    def pair_send(layer):
        SB[layer, :, :] = G[layer, span(other * hk, hk), :].astype(bf16)
        d = copy(("pair", layer), SB.at[layer], RB.at[layer], partner)
        d.start()
        pending.append(d)
        return d

    def across_x(layer, d):
        d.wait_recv()
        there = (1 - x) * qk
        XB[layer] = (
            G[layer, span(c * hk + there, qk), :] + RB[layer, span(there, qk), :].astype(f32)
        ).astype(bf16)
        d = copy(("x", layer), XB.at[layer], XR.at[layer], (y, z, (1 - x) * CORES + c))
        d.start()
        pending.append(d)
        return d

    def scatter(layer, d):
        here = x * qk
        both = G[layer, span(c * hk + here, qk), :] + RB[layer, span(here, qk), :].astype(f32)
        d.wait_recv()
        both = (both + XR[layer].astype(f32)).astype(bf16)
        for k in range(Z):
            PB[layer, k, 0:piece, :] = both[k * piece : (k + 1) * piece, :]
        found = []
        for j in range(1, Z):
            to = (z + j) % Z
            d = copy(("rs", layer, j), PB.at[layer, to], RP.at[layer, j - 1], (y, to, s))
            d.start()
            pending.append(d)
            found.append(d)
        return found

    def give(layer):
        at = OB.at[1 - layer, z]
        return copy("give", FB.at[layer], at, (y, z, layer * CORES + c))

    def along_z(which, dz):
        at = OB.at[which, z]
        return copy(("ag", which, dz), at, at, (y, (z + dz) % Z, s))

    def gather(layer, found):
        total = PB[layer, z].astype(f32)
        for j, d in enumerate(found):
            d.wait_recv()
            total = total + RP[layer, j].astype(f32)
        result = (total * grad_scale).astype(bf16)

        @pl.when(x == layer)
        def _():
            OB[layer, z] = result
            for dz in range(1, Z):
                along_z(layer, dz).start()

        @pl.when(x != layer)
        def _():
            FB[layer] = result
            give(layer).start()

    def pass_on(layer):
        @pl.when(x == layer)
        def _():
            give(layer).wait_recv()
            for dz in range(1, Z):
                along_z(1 - layer, dz).start()

    def collect(layer):
        @pl.when(x == layer)
        def _():
            for which in range(2):
                for dz in range(1, Z):
                    along_z(which, dz).wait_recv()
            for which in range(2):
                for k in range(Z):
                    row = which * qk + k * piece
                    wg[row : row + piece, :] = OB[which, k, 0:piece, :].astype(f32)
            for which in range(2):
                for dz in range(1, Z):
                    along_z(which, dz).wait_send()

        pl.when(x != layer)(give(layer).wait_send)

    grads(1, H, 2, D2)
    if fused:
        pair_two = pair_send(1)

    for p in range(CHUNKS):
        halo_wait("hd", D2, 2, p)

        def back_two(start):
            total = CT[p, span(start, tile), :].astype(f32) + jnp.dot(
                three(D2, p, 2, start, True), WT[K : 2 * K, :], preferred_element_type=f32
            )
            B1[p, span(start, tile), :] = total
            D1[p, span(start + mp, tile), :] = (total * SL[p, span(start, tile), :]).astype(bf16)

        tiles(back_two)
        halo_send("he", D1, 1, p)

    def finish(p):
        halo_wait("he", D1, 1, p)

        def back_one(start):
            OG[p, span(start, tile), :] = (
                B1[p, span(start, tile), :]
                + jnp.dot(three(D1, p, 1, start, True), WT[0:K, :], preferred_element_type=f32)
            ).astype(bf16)

        tiles(back_one)
        for j in range(1, S):
            to = (s + j) % S
            d = copy(
                ("o", p, j), OG.at[p, span(to * mp, mp)], out.at[span(s * m + p * mp, mp)],
                (y, z, to),
            )
            d.start()
            pending.append(d)
        out[span(s * m + p * mp, mp), :] = OG[p, span(s * mp, mp), :]

    if fused:
        cross_two = across_x(1, pair_two)
    for p in range(CHUNKS // 2):
        finish(p)
    grads(0, A, 1, D1)
    if fused:
        pair_one = pair_send(0)
        found_two = scatter(1, cross_two)
        cross_one = across_x(0, pair_one)
    for p in range(CHUNKS // 2, CHUNKS):
        finish(p)
    if fused:
        gather(1, found_two)
        found_one = scatter(0, cross_one)
        pass_on(1)
        gather(0, found_one)
        pass_on(0)
        collect(1)
        collect(0)
    else:
        wg[...] = G[...].reshape(2 * K, C)

    for p in range(CHUNKS):
        for j in range(1, S):
            came = out.at[span(((s + S - j) % S) * m + p * mp, mp)]
            copy(("o", p, j), came, came, partner).wait_recv()
    for d in pending:
        d.wait_send()
    for kind, buf, width, p in halos:
        up, down = halo_pair(kind, buf, width, p)
        pl.when(z < Z - 1)(up.wait_send)
        pl.when(z > 0)(down.wait_send)


def per_device(groups, Z, S, activations, cotangent, weights):
    n, C = activations.shape
    assert n == DILATION_FIRST and 2 * n == DILATION_SECOND and groups == 2 and S >= 2 * CORES
    K = 3 * C
    X = S // CORES
    mp = n // S // CHUNKS
    rows = n // CHUNKS
    fused = X == 2 and (K // 4) % (8 * Z) == 0 and (K // 4) % PAD == 0
    piece = K // 4 // Z if fused else PAD
    padded = -(-piece // PAD) * PAD
    pieces = Z if fused else 2
    qk = K // 4 if fused else PAD
    hk = K // 2 if fused else PAD
    bf16, f32 = jnp.bfloat16, jnp.float32
    semaphores = (S - 1) * CHUNKS * 3 + 8 * CHUNKS + 1 + 8 * X + 2 * (2 + Z) + 1 + 2 * Z + 8
    vmem = pl.BlockSpec(memory_space=pltpu.VMEM)
    input_grad, grads = pl.pallas_call(
        functools.partial(kernel, groups, Z, S, fused),
        out_shape=(
            jax.ShapeDtypeStruct((n, C), bf16),
            jax.ShapeDtypeStruct((weights.shape[0] if fused else 2 * K, C), f32),
        ),
        in_specs=[pl.BlockSpec(memory_space=pltpu.HBM)] * 3,
        out_specs=(vmem, vmem),
        scratch_shapes=[
            pltpu.VMEM((CHUNKS, rows + 2 * mp, C), bf16),
            pltpu.VMEM((CHUNKS, rows, C), bf16),
            pltpu.VMEM((CHUNKS, rows + 4 * mp, C), bf16),
            pltpu.VMEM((CHUNKS, rows + 4 * mp, C), bf16),
            pltpu.VMEM((CHUNKS, rows + 2 * mp, C), bf16),
            pltpu.VMEM((CHUNKS, rows, C), f32),
            pltpu.VMEM((CHUNKS, rows, C), f32),
            pltpu.VMEM((CHUNKS, rows, C), bf16),
            pltpu.VMEM((2 * K, C), bf16),
            pltpu.VMEM((2 * K, C), bf16),
            pltpu.VMEM((2, K, C), f32),
            pltpu.VMEM((2, hk, C), bf16),
            pltpu.VMEM((2, hk, C), bf16),
            pltpu.VMEM((2, qk, C), bf16),
            pltpu.VMEM((2, qk, C), bf16),
            pltpu.VMEM((2, pieces, padded, C), bf16),
            pltpu.VMEM((2, pieces - 1, padded, C), bf16),
            pltpu.VMEM((2, padded, C), bf16),
            pltpu.VMEM((2, pieces, padded, C), bf16),
            pltpu.SemaphoreType.DMA((semaphores,)),
            pltpu.SemaphoreType.DMA((semaphores,)),
            pltpu.SemaphoreType.DMA((2 * CHUNKS + 1,)),
        ],
        compiler_params=pltpu.CompilerParams(
            collective_id=0, has_side_effects=True, vmem_limit_bytes=62 * 1024 * 1024
        ),
        name="layers_backward",
    )(activations, cotangent, weights)
    if not fused:
        scale = 1.0 / math.sqrt(n * S * Z)
        grads = lax.psum(grads * scale, "seq")
        grads = lax.psum_scatter(grads, "sub", scatter_dimension=0, tiled=True)
    return (input_grad, grads)


def solution(mesh):
    placed = (P(("grp", "seq", "sub"), None), P(("grp", "seq", "sub"), None), P("sub", None))
    sizes = [mesh.shape[axis] for axis in ("grp", "seq", "sub")]
    return jax.shard_map(
        functools.partial(per_device, *sizes),
        mesh=mesh,
        in_specs=placed,
        out_specs=(P(("grp", "seq", "sub"), None), P(("grp", "sub"), None)),
        check_vma=False,
    )
```

```python
import functools
import math

import jax
import jax.numpy as jnp
from jax import lax
from jax.experimental import pallas as pl
from jax.experimental.pallas import tpu as pltpu
from jax.sharding import PartitionSpec as P

DILATION_FIRST = 1024
DILATION_SECOND = 2048
MESH = pl.DeviceIdType.MESH
CORES = 2
CHUNKS = 2
PAD = 16


def gelu_pair(pre_act):
    coeff = 0.7978845608
    tanh_value = jnp.tanh(coeff * (pre_act + 0.044715 * pre_act * pre_act * pre_act))
    gelu_value = 0.5 * pre_act * (1.0 + tanh_value)
    gelu_slope = 0.5 * (1.0 + tanh_value) + 0.5 * pre_act * (
        1.0 - tanh_value * tanh_value
    ) * coeff * (1.0 + 3.0 * 0.044715 * pre_act * pre_act)
    return (gelu_value, gelu_slope)


def kernel(
    groups, Z, S, fused, act, cot, wts, out, wg,
    A, CT, H, D2, D1, SL, B1, OG, W, WT, G, SB, RB, XB, XR, PB, RP, FB, OB, ssem, rsem, lsem,
):
    n, C = act.shape
    K = 3 * C
    X = S // CORES
    m = n // S
    mp = m // CHUNKS
    rows = n // CHUNKS
    tile = min(256, rows)
    y, z, s = lax.axis_index("grp"), lax.axis_index("seq"), lax.axis_index("sub")
    x, c = s // CORES, s % CORES
    other = 1 - c
    grad_scale = 1.0 / math.sqrt(n * S * Z)
    f32, bf16 = jnp.float32, jnp.bfloat16

    slots = {}

    def copy(name, src, dst, where):
        i = slots.setdefault(name, len(slots))
        return pltpu.make_async_remote_copy(
            src_ref=src, dst_ref=dst, send_sem=ssem.at[i], recv_sem=rsem.at[i],
            device_id=where, device_id_type=MESH,
        )

    def span(start, size):
        return pl.ds(pl.multiple_of(start, 16), size)

    pending = []
    local = {}

    def bring(name, src, dst):
        local[name] = pltpu.make_async_copy(src, dst, lsem.at[len(local)])
        local[name].start()

    barrier = pltpu.get_barrier_semaphore()
    greeted = 0

    def greet(where):
        pl.semaphore_signal(barrier, inc=1, device_id=where, device_id_type=MESH)

    for j in range(1, S):
        greet((y, z, (s + j) % S))
        greeted += 1
    for j in range(1, Z):
        greet((y, (z + j) % Z, s))
        greeted += 1
    greet((1 - y, z, s))
    greeted += 1
    pl.semaphore_wait(barrier, greeted)

    w = wts.shape[0]
    zs = 2 if Z % 2 == 0 and w % (4 * PAD) == 0 else 1
    pw = w // (2 * zs)
    h = z % zs
    partner = (y, z, x * CORES + other)
    beside = (y, z + 1 - 2 * h, s)
    across = (1 - y, z, s)

    def piece_of(shard, group, which):
        return W.at[span(shard * w + (group * zs + which) * pw, pw)]

    for j in range(1, X):
        d = copy(
            ("wx", j), wts.at[span((y * zs + h) * pw, pw)], piece_of(s, y, h),
            (y, z, ((x + j) % X) * CORES + c),
        )
        d.start()
        pending.append(d)
    d = copy("wc", wts, W.at[span(s * w, w)], partner)
    d.start()
    pending.append(d)

    def spread(kind, source, target, lead, p):
        found = []
        for j in range(1, S):
            to = (s + j) % S
            d = copy(
                (kind, p, j), source.at[span(to * m + p * mp, mp)],
                target.at[p, span((lead + s) * mp, mp)], (y, z, to),
            )
            d.start()
            pending.append(d)
            found.append(d)
        bring(
            (kind, p), source.at[span(s * m + p * mp, mp)],
            target.at[p, span((lead + s) * mp, mp)],
        )
        return found

    acts = [spread("a", act, A, 1, 0)]
    bring("w", wts, W.at[span(s * w, w)])

    def edges(buf, width):
        size = width * mp

        @pl.when(z == 0)
        def _():
            for p in range(CHUNKS):
                buf[p, 0:size, :] = jnp.zeros((size, C), bf16)

        @pl.when(z == Z - 1)
        def _():
            for p in range(CHUNKS):
                buf[p, size + rows : 2 * size + rows, :] = jnp.zeros((size, C), bf16)

    edges(A, 1)
    edges(H, 2)
    edges(D2, 2)
    edges(D1, 1)
    if fused:
        PB[...] = jnp.zeros(PB.shape, bf16)

    halos = []

    def halo_pair(kind, buf, width, p):
        size = width * mp
        up = copy(
            (kind, "up", p), buf.at[p, pl.ds(rows, size)], buf.at[p, pl.ds(0, size)],
            (y, jnp.minimum(z + 1, Z - 1), s),
        )
        down = copy(
            (kind, "down", p), buf.at[p, pl.ds(size, size)], buf.at[p, pl.ds(size + rows, size)],
            (y, jnp.maximum(z - 1, 0), s),
        )
        return up, down

    def halo_send(kind, buf, width, p):
        up, down = halo_pair(kind, buf, width, p)

        @pl.when(z < Z - 1)
        def _():
            up.start()

        @pl.when(z > 0)
        def _():
            down.start()

        halos.append((kind, buf, width, p))

    def halo_wait(kind, buf, width, p):
        up, down = halo_pair(kind, buf, width, p)

        @pl.when(z > 0)
        def _():
            up.wait_recv()

        @pl.when(z < Z - 1)
        def _():
            down.wait_recv()

    def forward(name, ref, where):
        d = copy(name, ref, ref, where)
        d.start()
        pending.append(d)

    def arrived(name, ref):
        copy(name, ref, ref, partner).wait_recv()

    for j in range(1, X):
        source = ((x + X - j) % X) * CORES + c
        mine = piece_of(source, y, h)
        arrived(("wx", j), mine)
        if zs == 2:
            forward(("wz", j), mine, beside)
        forward(("wy", j, 0), mine, across)
        forward(("wca", j, 0), mine, partner)
    acts += [spread("a", act, A, 1, p) for p in range(1, CHUNKS)]

    def edges_out(p):
        local["a", p].wait()
        for d in acts[p]:
            d.wait_recv()
        halo_send("ha", A, 1, p)

    edges_out(0)
    for j in range(1, X) if zs == 2 else ():
        source = ((x + X - j) % X) * CORES + c
        theirs = piece_of(source, y, 1 - h)
        arrived(("wz", j), theirs)
        forward(("wy", j, 1), theirs, across)
        forward(("wca", j, 1), theirs, partner)
    for p in range(1, CHUNKS):
        edges_out(p)
    for j in range(1, X):
        source = ((x + X - j) % X) * CORES + c
        for i in range(zs):
            theirs = piece_of(source, 1 - y, (h + i) % zs)
            arrived(("wy", j, i), theirs)
            forward(("wcb", j, i), theirs, partner)

    cots = [spread("c", cot, CT, 0, p) for p in range(CHUNKS)]

    local["w"].wait()
    pending[X - 1].wait_recv()
    for j in range(1, X):
        source = ((x + X - j) % X) * CORES + other
        for i in range(zs):
            arrived(("wca", j, i), piece_of(source, y, (h + i) % zs))
            arrived(("wcb", j, i), piece_of(source, 1 - y, (h + i) % zs))

    def three(buf, p, width, start, back):
        taps = [buf[p, span(start + k * width * mp, tile), :] for k in range(3)]
        return jnp.concatenate(taps[::-1] if back else taps, 1)

    def tiles(body):
        def step(t, carry):
            body(t * tile)
            return carry

        lax.fori_loop(0, rows // tile, step, 0)

    for p in range(CHUNKS):
        halo_wait("ha", A, 1, p)

        def layer_one(start):
            pre = jnp.dot(three(A, p, 1, start, False), W[0:K, :], preferred_element_type=f32)
            value, slope = gelu_pair(pre)
            SL[p, span(start, tile), :] = slope
            own = A[p, span(start + mp, tile), :].astype(f32)
            H[p, span(start + 2 * mp, tile), :] = (own + value).astype(bf16)

        tiles(layer_one)
        halo_send("hh", H, 2, p)

    for k in range(6):
        WT[k * C : (k + 1) * C, :] = W[k * C : (k + 1) * C, :].T

    for p in range(CHUNKS):
        local["c", p].wait()
        for d in cots[p]:
            d.wait_recv()
        halo_wait("hh", H, 2, p)

        def layer_two(start):
            pre = jnp.dot(three(H, p, 2, start, False), W[K : 2 * K, :], preferred_element_type=f32)
            slope = gelu_pair(pre)[1]
            here = CT[p, span(start, tile), :].astype(f32)
            D2[p, span(start + 2 * mp, tile), :] = (here * slope).astype(bf16)

        tiles(layer_two)
        halo_send("hd", D2, 2, p)

    def grads(layer, buf, width, delta):
        right = jnp.concatenate(
            [delta[p, width * mp : width * mp + rows, :] for p in range(CHUNKS)], 0
        )
        for k in range(3):
            start = k * width * mp
            left = jnp.concatenate([buf[p, start : start + rows, :] for p in range(CHUNKS)], 0)
            G[layer, k * C : (k + 1) * C, :] = lax.dot_general(
                left, right, (((0,), (0,)), ((), ())), preferred_element_type=f32
            )

    hk = K // 2
    qk = hk // 2
    piece = qk // Z

    def pair_send(layer):
        SB[layer, :, :] = G[layer, span(other * hk, hk), :].astype(bf16)
        d = copy(("pair", layer), SB.at[layer], RB.at[layer], partner)
        d.start()
        pending.append(d)
        return d

    def across_x(layer, d):
        d.wait_recv()
        there = (1 - x) * qk
        XB[layer] = (
            G[layer, span(c * hk + there, qk), :] + RB[layer, span(there, qk), :].astype(f32)
        ).astype(bf16)
        d = copy(("x", layer), XB.at[layer], XR.at[layer], (y, z, (1 - x) * CORES + c))
        d.start()
        pending.append(d)
        return d

    def scatter(layer, d):
        here = x * qk
        both = G[layer, span(c * hk + here, qk), :] + RB[layer, span(here, qk), :].astype(f32)
        d.wait_recv()
        both = (both + XR[layer].astype(f32)).astype(bf16)
        for k in range(Z):
            PB[layer, k, 0:piece, :] = both[k * piece : (k + 1) * piece, :]
        found = []
        for j in range(1, Z):
            to = (z + j) % Z
            d = copy(("rs", layer, j), PB.at[layer, to], RP.at[layer, j - 1], (y, to, s))
            d.start()
            pending.append(d)
            found.append(d)
        return found

    def give(layer):
        at = OB.at[1 - layer, z]
        return copy("give", FB.at[layer], at, (y, z, layer * CORES + c))

    def along_z(which, dz):
        at = OB.at[which, z]
        return copy(("ag", which, dz), at, at, (y, (z + dz) % Z, s))

    def gather(layer, found):
        total = PB[layer, z].astype(f32)
        for j, d in enumerate(found):
            d.wait_recv()
            total = total + RP[layer, j].astype(f32)
        result = (total * grad_scale).astype(bf16)

        @pl.when(x == layer)
        def _():
            OB[layer, z] = result
            for dz in range(1, Z):
                along_z(layer, dz).start()

        @pl.when(x != layer)
        def _():
            FB[layer] = result
            give(layer).start()

    def pass_on(layer):
        @pl.when(x == layer)
        def _():
            give(layer).wait_recv()
            for dz in range(1, Z):
                along_z(1 - layer, dz).start()

    def collect(layer):
        @pl.when(x == layer)
        def _():
            for which in range(2):
                for dz in range(1, Z):
                    along_z(which, dz).wait_recv()
            for which in range(2):
                for k in range(Z):
                    row = which * qk + k * piece
                    wg[row : row + piece, :] = OB[which, k, 0:piece, :].astype(f32)
            for which in range(2):
                for dz in range(1, Z):
                    along_z(which, dz).wait_send()

        pl.when(x != layer)(give(layer).wait_send)

    grads(1, H, 2, D2)
    if fused:
        pair_two = pair_send(1)

    for p in range(CHUNKS):
        halo_wait("hd", D2, 2, p)

        def back_two(start):
            total = CT[p, span(start, tile), :].astype(f32) + jnp.dot(
                three(D2, p, 2, start, True), WT[K : 2 * K, :], preferred_element_type=f32
            )
            B1[p, span(start, tile), :] = total
            D1[p, span(start + mp, tile), :] = (total * SL[p, span(start, tile), :]).astype(bf16)

        tiles(back_two)
        halo_send("he", D1, 1, p)

    def finish(p):
        halo_wait("he", D1, 1, p)

        def back_one(start):
            OG[p, span(start, tile), :] = (
                B1[p, span(start, tile), :]
                + jnp.dot(three(D1, p, 1, start, True), WT[0:K, :], preferred_element_type=f32)
            ).astype(bf16)

        tiles(back_one)

    def give_out(p):
        for j in range(1, S):
            to = (s + j) % S
            d = copy(
                ("o", p, j), OG.at[p, span(to * mp, mp)], out.at[span(s * m + p * mp, mp)],
                (y, z, to),
            )
            d.start()
            pending.append(d)
        out[span(s * m + p * mp, mp), :] = OG[p, span(s * mp, mp), :]

    if fused:
        cross_two = across_x(1, pair_two)
    grads(0, A, 1, D1)
    if fused:
        pair_one = pair_send(0)
        found_two = scatter(1, cross_two)
        cross_one = across_x(0, pair_one)
    finish(0)
    if fused:
        found_one = scatter(0, cross_one)
    give_out(0)
    if fused:
        gather(1, found_two)
    for p in range(1, CHUNKS):
        finish(p)
        give_out(p)
    if fused:
        gather(0, found_one)
        pass_on(1)
        pass_on(0)
        collect(1)
        collect(0)
    else:
        wg[...] = G[...].reshape(2 * K, C)

    for p in range(CHUNKS):
        for j in range(1, S):
            came = out.at[span(((s + S - j) % S) * m + p * mp, mp)]
            copy(("o", p, j), came, came, partner).wait_recv()
    for d in pending:
        d.wait_send()
    for kind, buf, width, p in halos:
        up, down = halo_pair(kind, buf, width, p)
        pl.when(z < Z - 1)(up.wait_send)
        pl.when(z > 0)(down.wait_send)


def per_device(groups, Z, S, activations, cotangent, weights):
    n, C = activations.shape
    assert n == DILATION_FIRST and 2 * n == DILATION_SECOND and groups == 2 and S >= 2 * CORES
    K = 3 * C
    X = S // CORES
    mp = n // S // CHUNKS
    rows = n // CHUNKS
    fused = X == 2 and (K // 4) % (8 * Z) == 0 and (K // 4) % PAD == 0
    piece = K // 4 // Z if fused else PAD
    padded = -(-piece // PAD) * PAD
    pieces = Z if fused else 2
    qk = K // 4 if fused else PAD
    hk = K // 2 if fused else PAD
    bf16, f32 = jnp.bfloat16, jnp.float32
    semaphores = (S - 1) * CHUNKS * 3 + 8 * CHUNKS + 1 + 8 * X + 2 * (2 + Z) + 1 + 2 * Z + 8
    vmem = pl.BlockSpec(memory_space=pltpu.VMEM)
    input_grad, grads = pl.pallas_call(
        functools.partial(kernel, groups, Z, S, fused),
        out_shape=(
            jax.ShapeDtypeStruct((n, C), bf16),
            jax.ShapeDtypeStruct((weights.shape[0] if fused else 2 * K, C), f32),
        ),
        in_specs=[pl.BlockSpec(memory_space=pltpu.HBM)] * 3,
        out_specs=(vmem, vmem),
        scratch_shapes=[
            pltpu.VMEM((CHUNKS, rows + 2 * mp, C), bf16),
            pltpu.VMEM((CHUNKS, rows, C), bf16),
            pltpu.VMEM((CHUNKS, rows + 4 * mp, C), bf16),
            pltpu.VMEM((CHUNKS, rows + 4 * mp, C), bf16),
            pltpu.VMEM((CHUNKS, rows + 2 * mp, C), bf16),
            pltpu.VMEM((CHUNKS, rows, C), f32),
            pltpu.VMEM((CHUNKS, rows, C), f32),
            pltpu.VMEM((CHUNKS, rows, C), bf16),
            pltpu.VMEM((2 * K, C), bf16),
            pltpu.VMEM((2 * K, C), bf16),
            pltpu.VMEM((2, K, C), f32),
            pltpu.VMEM((2, hk, C), bf16),
            pltpu.VMEM((2, hk, C), bf16),
            pltpu.VMEM((2, qk, C), bf16),
            pltpu.VMEM((2, qk, C), bf16),
            pltpu.VMEM((2, pieces, padded, C), bf16),
            pltpu.VMEM((2, pieces - 1, padded, C), bf16),
            pltpu.VMEM((2, padded, C), bf16),
            pltpu.VMEM((2, pieces, padded, C), bf16),
            pltpu.SemaphoreType.DMA((semaphores,)),
            pltpu.SemaphoreType.DMA((semaphores,)),
            pltpu.SemaphoreType.DMA((2 * CHUNKS + 1,)),
        ],
        compiler_params=pltpu.CompilerParams(
            collective_id=0, has_side_effects=True, vmem_limit_bytes=48 * 1024 * 1024
        ),
        name="layers_backward",
    )(activations, cotangent, weights)
    if not fused:
        scale = 1.0 / math.sqrt(n * S * Z)
        grads = lax.psum(grads * scale, "seq")
        grads = lax.psum_scatter(grads, "sub", scatter_dimension=0, tiled=True)
    return (input_grad, grads)


def solution(mesh):
    placed = (P(("grp", "seq", "sub"), None), P(("grp", "seq", "sub"), None), P("sub", None))
    sizes = [mesh.shape[axis] for axis in ("grp", "seq", "sub")]
    return jax.shard_map(
        functools.partial(per_device, *sizes),
        mesh=mesh,
        in_specs=placed,
        out_specs=(P(("grp", "seq", "sub"), None), P(("grp", "sub"), None)),
        check_vma=False,
    )
```

```python
import functools
import math

import jax
import jax.numpy as jnp
from jax import lax
from jax.experimental import pallas as pl
from jax.experimental.pallas import tpu as pltpu
from jax.sharding import PartitionSpec as P

DILATION_FIRST = 1024
DILATION_SECOND = 2048
MESH = pl.DeviceIdType.MESH
CORES = 2
CHUNKS = 2
PAD = 16


def gelu_pair(pre_act):
    coeff = 0.7978845608
    tanh_value = jnp.tanh(coeff * (pre_act + 0.044715 * pre_act * pre_act * pre_act))
    gelu_value = 0.5 * pre_act * (1.0 + tanh_value)
    gelu_slope = 0.5 * (1.0 + tanh_value) + 0.5 * pre_act * (
        1.0 - tanh_value * tanh_value
    ) * coeff * (1.0 + 3.0 * 0.044715 * pre_act * pre_act)
    return (gelu_value, gelu_slope)


def kernel(
    groups, Z, S, fused, act, cot, wts, out, wg,
    A, CT, H, D2, D1, SL, B1, OG, W, WT, G, SB, RB, XB, XR, PB, RP, FB, OB, ssem, rsem, lsem,
):
    n, C = act.shape
    K = 3 * C
    X = S // CORES
    m = n // S
    mp = m // CHUNKS
    rows = n // CHUNKS
    tile = min(256, rows)
    y, z, s = lax.axis_index("grp"), lax.axis_index("seq"), lax.axis_index("sub")
    x, c = s // CORES, s % CORES
    other = 1 - c
    grad_scale = 1.0 / math.sqrt(n * S * Z)
    f32, bf16 = jnp.float32, jnp.bfloat16

    slots = {}

    def copy(name, src, dst, where):
        i = slots.setdefault(name, len(slots))
        return pltpu.make_async_remote_copy(
            src_ref=src, dst_ref=dst, send_sem=ssem.at[i], recv_sem=rsem.at[i],
            device_id=where, device_id_type=MESH,
        )

    def span(start, size):
        return pl.ds(pl.multiple_of(start, 16), size)

    pending = []
    local = {}

    def bring(name, src, dst):
        local[name] = pltpu.make_async_copy(src, dst, lsem.at[len(local)])
        local[name].start()

    barrier = pltpu.get_barrier_semaphore()
    greeted = 0

    def greet(where):
        pl.semaphore_signal(barrier, inc=1, device_id=where, device_id_type=MESH)

    for j in range(1, S):
        greet((y, z, (s + j) % S))
        greeted += 1
    for j in range(1, Z):
        greet((y, (z + j) % Z, s))
        greeted += 1
    greet((1 - y, z, s))
    greeted += 1
    pl.semaphore_wait(barrier, greeted)

    w = wts.shape[0]
    hw = w // 2
    partner = (y, z, x * CORES + other)

    def half(shard, which):
        return W.at[span((shard * 2 + which) * hw, hw)]

    for j in range(1, X):
        d = copy(("wx", j), wts.at[span(y * hw, hw)], half(s, y), (y, z, ((x + j) % X) * CORES + c))
        d.start()
        pending.append(d)
    d = copy("wc", wts, W.at[span(s * w, w)], partner)
    d.start()
    pending.append(d)

    def spread(kind, source, target, lead, p):
        found = []
        for j in range(1, S):
            to = (s + j) % S
            d = copy(
                (kind, p, j), source.at[span(to * m + p * mp, mp)],
                target.at[p, span((lead + s) * mp, mp)], (y, z, to),
            )
            d.start()
            pending.append(d)
            found.append(d)
        bring(
            (kind, p), source.at[span(s * m + p * mp, mp)],
            target.at[p, span((lead + s) * mp, mp)],
        )
        return found

    acts = [spread("a", act, A, 1, p) for p in range(CHUNKS)]
    bring("w", wts, W.at[span(s * w, w)])

    def edges(buf, width):
        size = width * mp

        @pl.when(z == 0)
        def _():
            for p in range(CHUNKS):
                buf[p, 0:size, :] = jnp.zeros((size, C), bf16)

        @pl.when(z == Z - 1)
        def _():
            for p in range(CHUNKS):
                buf[p, size + rows : 2 * size + rows, :] = jnp.zeros((size, C), bf16)

    edges(A, 1)
    edges(H, 2)
    edges(D2, 2)
    edges(D1, 1)
    if fused:
        PB[...] = jnp.zeros(PB.shape, bf16)

    halos = []

    def halo_pair(kind, buf, width, p):
        size = width * mp
        up = copy(
            (kind, "up", p), buf.at[p, pl.ds(rows, size)], buf.at[p, pl.ds(0, size)],
            (y, jnp.minimum(z + 1, Z - 1), s),
        )
        down = copy(
            (kind, "down", p), buf.at[p, pl.ds(size, size)], buf.at[p, pl.ds(size + rows, size)],
            (y, jnp.maximum(z - 1, 0), s),
        )
        return up, down

    def halo_send(kind, buf, width, p):
        up, down = halo_pair(kind, buf, width, p)

        @pl.when(z < Z - 1)
        def _():
            up.start()

        @pl.when(z > 0)
        def _():
            down.start()

        halos.append((kind, buf, width, p))

    def halo_wait(kind, buf, width, p):
        up, down = halo_pair(kind, buf, width, p)

        @pl.when(z > 0)
        def _():
            up.wait_recv()

        @pl.when(z < Z - 1)
        def _():
            down.wait_recv()

    forwards = []
    for j in range(1, X):
        source = ((x + X - j) % X) * CORES + c
        copy(("wx", j), half(source, y), half(source, y), partner).wait_recv()
        d = copy(("wy", j), half(source, y), half(source, y), (1 - y, z, s))
        d.start()
        pending.append(d)
        d = copy(("wca", j), half(source, y), half(source, y), partner)
        d.start()
        pending.append(d)
    for j in range(1, X):
        source = ((x + X - j) % X) * CORES + c
        theirs = half(source, 1 - y)
        copy(("wy", j), theirs, theirs, partner).wait_recv()
        d = copy(("wcb", j), theirs, theirs, partner)
        d.start()
        pending.append(d)

    for p in range(CHUNKS):
        local["a", p].wait()
        for d in acts[p]:
            d.wait_recv()
        halo_send("ha", A, 1, p)
    cots = [spread("c", cot, CT, 0, p) for p in range(CHUNKS)]

    local["w"].wait()
    pending[X - 1].wait_recv()
    for j in range(1, X):
        source = ((x + X - j) % X) * CORES + other
        copy(("wca", j), half(source, y), half(source, y), partner).wait_recv()
        copy(("wcb", j), half(source, 1 - y), half(source, 1 - y), partner).wait_recv()

    def three(buf, p, width, start, back):
        taps = [buf[p, span(start + k * width * mp, tile), :] for k in range(3)]
        return jnp.concatenate(taps[::-1] if back else taps, 1)

    def tiles(body):
        def step(t, carry):
            body(t * tile)
            return carry

        lax.fori_loop(0, rows // tile, step, 0)

    for p in range(CHUNKS):
        halo_wait("ha", A, 1, p)

        def layer_one(start):
            pre = jnp.dot(three(A, p, 1, start, False), W[0:K, :], preferred_element_type=f32)
            value, slope = gelu_pair(pre)
            SL[p, span(start, tile), :] = slope
            own = A[p, span(start + mp, tile), :].astype(f32)
            H[p, span(start + 2 * mp, tile), :] = (own + value).astype(bf16)

        tiles(layer_one)
        halo_send("hh", H, 2, p)

    for k in range(6):
        WT[k * C : (k + 1) * C, :] = W[k * C : (k + 1) * C, :].T

    for p in range(CHUNKS):
        local["c", p].wait()
        for d in cots[p]:
            d.wait_recv()
        halo_wait("hh", H, 2, p)

        def layer_two(start):
            pre = jnp.dot(three(H, p, 2, start, False), W[K : 2 * K, :], preferred_element_type=f32)
            slope = gelu_pair(pre)[1]
            here = CT[p, span(start, tile), :].astype(f32)
            D2[p, span(start + 2 * mp, tile), :] = (here * slope).astype(bf16)

        tiles(layer_two)
        halo_send("hd", D2, 2, p)

    def grads(layer, buf, width, delta):
        for k in range(3):
            total = None
            for p in range(CHUNKS):
                part = lax.dot_general(
                    buf[p, k * width * mp : k * width * mp + rows, :],
                    delta[p, width * mp : width * mp + rows, :],
                    (((0,), (0,)), ((), ())), preferred_element_type=f32,
                )
                total = part if total is None else total + part
            G[layer, k * C : (k + 1) * C, :] = total

    hk = K // 2
    qk = hk // 2
    piece = qk // Z

    def pair_send(layer):
        SB[layer, :, :] = G[layer, span(other * hk, hk), :].astype(bf16)
        d = copy(("pair", layer), SB.at[layer], RB.at[layer], partner)
        d.start()
        pending.append(d)
        return d

    def across_x(layer, d):
        d.wait_recv()
        there = (1 - x) * qk
        XB[layer] = (
            G[layer, span(c * hk + there, qk), :] + RB[layer, span(there, qk), :].astype(f32)
        ).astype(bf16)
        d = copy(("x", layer), XB.at[layer], XR.at[layer], (y, z, (1 - x) * CORES + c))
        d.start()
        pending.append(d)
        return d

    def scatter(layer, d):
        here = x * qk
        both = G[layer, span(c * hk + here, qk), :] + RB[layer, span(here, qk), :].astype(f32)
        d.wait_recv()
        both = (both + XR[layer].astype(f32)).astype(bf16)
        for k in range(Z):
            PB[layer, k, 0:piece, :] = both[k * piece : (k + 1) * piece, :]
        found = []
        for j in range(1, Z):
            to = (z + j) % Z
            d = copy(("rs", layer, j), PB.at[layer, to], RP.at[layer, j - 1], (y, to, s))
            d.start()
            pending.append(d)
            found.append(d)
        return found

    def give(layer):
        at = OB.at[1 - layer, z]
        return copy("give", FB.at[layer], at, (y, z, layer * CORES + c))

    def along_z(which, dz):
        at = OB.at[which, z]
        return copy(("ag", which, dz), at, at, (y, (z + dz) % Z, s))

    def gather(layer, found):
        total = PB[layer, z].astype(f32)
        for j, d in enumerate(found):
            d.wait_recv()
            total = total + RP[layer, j].astype(f32)
        result = (total * grad_scale).astype(bf16)

        @pl.when(x == layer)
        def _():
            OB[layer, z] = result
            for dz in range(1, Z):
                along_z(layer, dz).start()

        @pl.when(x != layer)
        def _():
            FB[layer] = result
            give(layer).start()

    def pass_on(layer):
        @pl.when(x == layer)
        def _():
            give(layer).wait_recv()
            for dz in range(1, Z):
                along_z(1 - layer, dz).start()

    def collect(layer):
        @pl.when(x == layer)
        def _():
            for which in range(2):
                for dz in range(1, Z):
                    along_z(which, dz).wait_recv()
            for which in range(2):
                for k in range(Z):
                    row = which * qk + k * piece
                    wg[row : row + piece, :] = OB[which, k, 0:piece, :].astype(f32)
            for which in range(2):
                for dz in range(1, Z):
                    along_z(which, dz).wait_send()

        pl.when(x != layer)(give(layer).wait_send)

    grads(1, H, 2, D2)
    if fused:
        pair_two = pair_send(1)

    for p in range(CHUNKS):
        halo_wait("hd", D2, 2, p)

        def back_two(start):
            total = CT[p, span(start, tile), :].astype(f32) + jnp.dot(
                three(D2, p, 2, start, True), WT[K : 2 * K, :], preferred_element_type=f32
            )
            B1[p, span(start, tile), :] = total
            D1[p, span(start + mp, tile), :] = (total * SL[p, span(start, tile), :]).astype(bf16)

        tiles(back_two)
        halo_send("he", D1, 1, p)

    if fused:
        cross_two = across_x(1, pair_two)
    grads(0, A, 1, D1)
    if fused:
        pair_one = pair_send(0)
        found_two = scatter(1, cross_two)
        cross_one = across_x(0, pair_one)

    for p in range(CHUNKS):
        halo_wait("he", D1, 1, p)

        def back_one(start):
            OG[p, span(start, tile), :] = (
                B1[p, span(start, tile), :]
                + jnp.dot(three(D1, p, 1, start, True), WT[0:K, :], preferred_element_type=f32)
            ).astype(bf16)

        tiles(back_one)
        if fused and p == 0:
            found_one = scatter(0, cross_one)
        if fused and p == CHUNKS - 1:
            gather(1, found_two)
        for j in range(1, S):
            to = (s + j) % S
            d = copy(
                ("o", p, j), OG.at[p, span(to * mp, mp)], out.at[span(s * m + p * mp, mp)],
                (y, z, to),
            )
            d.start()
            pending.append(d)
        out[span(s * m + p * mp, mp), :] = OG[p, span(s * mp, mp), :]

    if fused:
        pass_on(1)
        gather(0, found_one)
        pass_on(0)
        collect(1)
        collect(0)
    else:
        wg[...] = G[...].reshape(2 * K, C)

    for p in range(CHUNKS):
        for j in range(1, S):
            came = out.at[span(((s + S - j) % S) * m + p * mp, mp)]
            copy(("o", p, j), came, came, partner).wait_recv()
    for d in pending:
        d.wait_send()
    for kind, buf, width, p in halos:
        up, down = halo_pair(kind, buf, width, p)
        pl.when(z < Z - 1)(up.wait_send)
        pl.when(z > 0)(down.wait_send)


def per_device(groups, Z, S, activations, cotangent, weights):
    n, C = activations.shape
    assert n == DILATION_FIRST and 2 * n == DILATION_SECOND and groups == 2 and S >= 2 * CORES
    K = 3 * C
    X = S // CORES
    mp = n // S // CHUNKS
    rows = n // CHUNKS
    fused = X == 2 and (K // 4) % (8 * Z) == 0 and (K // 4) % PAD == 0
    piece = K // 4 // Z if fused else PAD
    padded = -(-piece // PAD) * PAD
    pieces = Z if fused else 2
    qk = K // 4 if fused else PAD
    hk = K // 2 if fused else PAD
    bf16, f32 = jnp.bfloat16, jnp.float32
    semaphores = (S - 1) * CHUNKS * 3 + 8 * CHUNKS + 1 + 4 * X + 2 * (2 + Z) + 1 + 2 * Z + 8
    vmem = pl.BlockSpec(memory_space=pltpu.VMEM)
    input_grad, grads = pl.pallas_call(
        functools.partial(kernel, groups, Z, S, fused),
        out_shape=(
            jax.ShapeDtypeStruct((n, C), bf16),
            jax.ShapeDtypeStruct((weights.shape[0] if fused else 2 * K, C), f32),
        ),
        in_specs=[pl.BlockSpec(memory_space=pltpu.HBM)] * 3,
        out_specs=(vmem, vmem),
        scratch_shapes=[
            pltpu.VMEM((CHUNKS, rows + 2 * mp, C), bf16),
            pltpu.VMEM((CHUNKS, rows, C), bf16),
            pltpu.VMEM((CHUNKS, rows + 4 * mp, C), bf16),
            pltpu.VMEM((CHUNKS, rows + 4 * mp, C), bf16),
            pltpu.VMEM((CHUNKS, rows + 2 * mp, C), bf16),
            pltpu.VMEM((CHUNKS, rows, C), f32),
            pltpu.VMEM((CHUNKS, rows, C), f32),
            pltpu.VMEM((CHUNKS, rows, C), bf16),
            pltpu.VMEM((2 * K, C), bf16),
            pltpu.VMEM((2 * K, C), bf16),
            pltpu.VMEM((2, K, C), f32),
            pltpu.VMEM((2, hk, C), bf16),
            pltpu.VMEM((2, hk, C), bf16),
            pltpu.VMEM((2, qk, C), bf16),
            pltpu.VMEM((2, qk, C), bf16),
            pltpu.VMEM((2, pieces, padded, C), bf16),
            pltpu.VMEM((2, pieces - 1, padded, C), bf16),
            pltpu.VMEM((2, padded, C), bf16),
            pltpu.VMEM((2, pieces, padded, C), bf16),
            pltpu.SemaphoreType.DMA((semaphores,)),
            pltpu.SemaphoreType.DMA((semaphores,)),
            pltpu.SemaphoreType.DMA((2 * CHUNKS + 1,)),
        ],
        compiler_params=pltpu.CompilerParams(
            collective_id=0, has_side_effects=True, vmem_limit_bytes=48 * 1024 * 1024
        ),
        name="layers_backward",
    )(activations, cotangent, weights)
    if not fused:
        scale = 1.0 / math.sqrt(n * S * Z)
        grads = lax.psum(grads * scale, "seq")
        grads = lax.psum_scatter(grads, "sub", scatter_dimension=0, tiled=True)
    return (input_grad, grads)


def solution(mesh):
    placed = (P(("grp", "seq", "sub"), None), P(("grp", "seq", "sub"), None), P("sub", None))
    sizes = [mesh.shape[axis] for axis in ("grp", "seq", "sub")]
    return jax.shard_map(
        functools.partial(per_device, *sizes),
        mesh=mesh,
        in_specs=placed,
        out_specs=(P(("grp", "seq", "sub"), None), P(("grp", "sub"), None)),
        check_vma=False,
    )
```
